32 devices in a mesh: slab: 8 (over z, y), brick: 4 (over x, core).
Axes of the slice: x: 2, y: 2, z: 4, core: 2. Of those that a mesh axis runs over, the one named last changes fastest.
Arguments:
- opening_warmth_values: float32 [16, 128, 512], P('slab', 'brick'), may hold values from -6 to 6
- thermal_diffusivity_field: float32 [16, 128, 512], P('slab', 'brick'), may hold values from 0.3 to 3
- atom_released_joules: float32 [8, 4, 8, 128], P('slab', 'brick'), may hold values from 0.1 to 1
- atom_local_coordinates: float32 [8, 4, 8, 3, 128], P('slab', 'brick'), may hold values from 0 to 1
- atom_anchor_voxel: int32 [8, 4, 8, 128], P('slab', 'brick'), may hold values from 0 to 15870, as said below
- atom_oxygen_flag: int32 [8, 4, 8, 128], P('slab', 'brick'), may hold values 0 or 1
- live_entries_number: int32 [8, 4, 8], P('slab', 'brick'), may hold values from 42 to 128, as said below
Outputs:
- advanced_warmth_values: float32 [16, 128, 512], P('slab', 'brick')
- probe_warmth_readout: float32 [8, 4, 8, 128], P('slab', 'brick')
The draws below stay inside these ranges and needn't reach their ends.
Inputs may be any that keep to these rules, and one draw needn't show every extreme that they name: `atom_anchor_voxel`: each slot's base cell has plane below 1, row below 31 and column below 511 of the owner's block, so all eight corners lie in that block. `live_entries_number`: for every brick index one owner slab receives 128 live slots from every source device; any slot count may be reached elsewhere within the range.
All inputs are finite; a program needn't handle non-finite values. No bound on the sum of `atom_oxygen_flag` on one device may be relied on, other than what follows from the above.
Results may differ from the reference program's by a relative error of at most 0.0003.
Values sent between devices are 32-bit elements; how exact they have to be, the bound alone decides.
A program may use at most 64 MiB of HBM per device.

```python
import math
import jax
import jax.numpy as jnp
from jax import lax

CZ = 2
CX = 32
MESH_COLUMNS = 512
CAP = 128
ITERS = 8
MESH_LAYERS = 16
MESH_LINES = 128
N_SLAB = 8
N_BRICK = 4


def draw_atom_anchor_voxel(key, part):
    key = jax.random.fold_in(key, 11)
    first, second, third = jax.random.split(key, 3)
    array_shape = (N_SLAB, N_BRICK, N_SLAB, CAP)
    plane_pick = jax.random.randint(first, array_shape, 0, CZ - 1, dtype=jnp.int32)
    row_pick = jax.random.randint(second, array_shape, 0, CX - 1, dtype=jnp.int32)
    column_pick = jax.random.randint(third, array_shape, 0, MESH_COLUMNS - 1, dtype=jnp.int32)
    return plane_pick * (CX * MESH_COLUMNS) + row_pick * MESH_COLUMNS + column_pick


def draw_live_entries_number(key, part):
    key = jax.random.fold_in(key, 23)
    first, second = jax.random.split(key, 2)
    base = jax.random.randint(first, (N_SLAB, N_BRICK, N_SLAB), CAP // 3, CAP * 2 // 3 + 1, dtype=jnp.int32)
    crowded = jax.random.randint(second, (1, N_BRICK, 1), 0, N_SLAB, dtype=jnp.int32)
    owners = jnp.arange(N_SLAB, dtype=jnp.int32).reshape(1, 1, N_SLAB)
    return jnp.where(owners == crowded, jnp.int32(CAP), base)


def with_ends(drawn, stream_key, low, high):
    index_at = [jax.random.randint(jax.random.fold_in(stream_key, axis), (), 0, length) for axis, length in enumerate(drawn.shape)]
    widest = drawn.shape.index(max(drawn.shape))
    next_to = index_at[:widest] + [(index_at[widest] + 1) % drawn.shape[widest]] + index_at[widest + 1:]
    return drawn.at[tuple(index_at)].set(low).at[tuple(next_to)].set(high)


def block_levels(own_key, shape, cuts, least, largest):
    level, own = 1.0, jax.random.fold_in(own_key, 6)
    for position, shards_of in cuts:
        steps = jnp.exp(jax.random.uniform(jax.random.fold_in(own, position), (shards_of,), jnp.float32, least / len(cuts), largest / len(cuts)))
        level = level * jnp.repeat(steps, shape[position] // shards_of).reshape([-1 if axis == position else 1 for axis in range(len(shape))])
    return level


def centred(stream_key, extent, deviation, reach, shards=(), kind=jnp.bfloat16):
    drawn = deviation * jax.random.normal(stream_key, extent, jnp.float32)
    if shards:
        drawn = drawn * block_levels(stream_key, extent, shards, -0.22, 0.18)
    return jnp.clip(drawn, -reach, reach).astype(kind)


def setup_inputs(seed: int = 0) -> dict:
    keys = jax.random.split(jax.random.key(seed), 8)
    return {
        "opening_warmth_values": centred(keys[0], (MESH_LAYERS, MESH_LINES, MESH_COLUMNS), 1.0, 6.0, ((0, 8), (1, 4)), jnp.float32),
        "thermal_diffusivity_field": jnp.clip(jnp.exp(math.log(3.0) - 2.3025851 * jax.random.uniform(keys[1], (MESH_LAYERS, MESH_LINES, MESH_COLUMNS), jnp.float32) ** block_levels(keys[1], (MESH_LAYERS, MESH_LINES, MESH_COLUMNS), ((0, 8), (1, 4)), -0.2, 0.2)), 0.3, 3.0),
        "atom_released_joules": jnp.clip(jnp.exp(math.log(1.0) - 2.3025851 * jax.random.uniform(keys[2], (N_SLAB, N_BRICK, N_SLAB, CAP), jnp.float32) ** block_levels(keys[2], (N_SLAB, N_BRICK, N_SLAB, CAP), ((0, 8), (1, 4)), -0.2, 0.2)), 0.1, 1.0),
        "atom_local_coordinates": jnp.clip(1.0 * jax.random.uniform(keys[3], (N_SLAB, N_BRICK, N_SLAB, 3, CAP), jnp.float32) ** block_levels(keys[3], (N_SLAB, N_BRICK, N_SLAB, 3, CAP), ((0, 8), (1, 4)), -0.2, 0.2), 0.0, 1.0),
        "atom_anchor_voxel": draw_atom_anchor_voxel(jax.random.fold_in(keys[7], 71), 0),
        "atom_oxygen_flag": with_ends((jax.random.randint(keys[5], (N_SLAB, N_BRICK, N_SLAB, CAP), 0, 3) < 1).astype(jnp.int32), jax.random.fold_in(keys[5], 1), 0, 1),
        "live_entries_number": draw_live_entries_number(jax.random.fold_in(keys[7], 71), 0),
    }


recombine_gain = 3.0
half_interval = 16.0
interval_length = 32.0


def adjacent_sites_list(padded):
    return [padded[:-2, 1:-1, 1:-1], padded[2:, 1:-1, 1:-1], padded[1:-1, :-2, 1:-1],
            padded[1:-1, 2:, 1:-1], padded[1:-1, 1:-1, :-2], padded[1:-1, 1:-1, 2:]]


def diffusion_matrix(field, coupling_coefficient, main_entry_accumulated):
    others = adjacent_sites_list(jnp.pad(field, 1))
    coupled = coupling_coefficient[0] * others[0]
    for index in range(1, 6):
        coupled = coupled + coupling_coefficient[index] * others[index]
    return main_entry_accumulated * field - coupled


def corner_list(frac_z, frac_x, frac_y):
    result = []
    for step_z in (0, 1):
        weight_z = frac_z if step_z else 1.0 - frac_z
        for step_x in (0, 1):
            weight_x = frac_x if step_x else 1.0 - frac_x
            for step_y in (0, 1):
                weight_y = frac_y if step_y else 1.0 - frac_y
                result.append((step_z, step_x, step_y, (weight_z * weight_x) * weight_y))
    return result


def reference(opening_warmth_values, thermal_diffusivity_field, atom_released_joules, atom_local_coordinates, atom_anchor_voxel, atom_oxygen_flag, live_entries_number):
    live = lax.broadcasted_iota(jnp.int32, atom_released_joules.shape, 3) < live_entries_number[..., None]
    heat = jnp.where(live, atom_released_joules * (1.0 + recombine_gain * atom_oxygen_flag.astype(jnp.float32)), 0.0)
    plane = CX * MESH_COLUMNS
    local_z = atom_anchor_voxel // plane
    local_x = (atom_anchor_voxel // MESH_COLUMNS) % CX
    local_y = atom_anchor_voxel % MESH_COLUMNS
    owner = lax.broadcasted_iota(jnp.int32, atom_anchor_voxel.shape, 2)
    column = lax.broadcasted_iota(jnp.int32, atom_anchor_voxel.shape, 1)
    base_z = owner * CZ + local_z
    base_x = column * CX + local_x
    corners = corner_list(atom_local_coordinates[:, :, :, 0, :], atom_local_coordinates[:, :, :, 1, :], atom_local_coordinates[:, :, :, 2, :])
    targets = []
    amounts = []
    for step_z, step_x, step_y, weight in corners:
        target = ((base_z + step_z) * MESH_LINES + base_x + step_x) * MESH_COLUMNS + local_y + step_y
        targets.append(target.astype(jnp.int32))
        amounts.append(heat * weight)
    flat_source = jnp.zeros((MESH_LAYERS * MESH_LINES * MESH_COLUMNS,), jnp.float32)
    flat_source = flat_source.at[jnp.concatenate([item.reshape(-1) for item in targets])].add(
        jnp.concatenate([item.reshape(-1) for item in amounts]))
    deposited_power = flat_source.reshape(MESH_LAYERS, MESH_LINES, MESH_COLUMNS)

    coupling_coefficient = [0.5 * (thermal_diffusivity_field + other) for other in adjacent_sites_list(jnp.pad(thermal_diffusivity_field, 1))]
    main_entry_accumulated = coupling_coefficient[0]
    for index in range(1, 6):
        main_entry_accumulated = main_entry_accumulated + coupling_coefficient[index]

    starting_contribution = diffusion_matrix(opening_warmth_values, coupling_coefficient, main_entry_accumulated)
    linear_system_load = opening_warmth_values - half_interval * starting_contribution + interval_length * deposited_power
    advanced_warmth_values = opening_warmth_values
    equation_mismatch = linear_system_load - (opening_warmth_values + half_interval * starting_contribution)
    compass_heading = equation_mismatch
    norm_now = jnp.sum(equation_mismatch * equation_mismatch)
    for step in range(ITERS):
        image = compass_heading + half_interval * diffusion_matrix(compass_heading, coupling_coefficient, main_entry_accumulated)
        implicit_blend = norm_now / jnp.sum(compass_heading * image)
        advanced_warmth_values = advanced_warmth_values + implicit_blend * compass_heading
        equation_mismatch = equation_mismatch - implicit_blend * image
        norm_next = jnp.sum(equation_mismatch * equation_mismatch)
        compass_heading = equation_mismatch + (norm_next / norm_now) * compass_heading
        norm_now = norm_next

    raveled_fresh = advanced_warmth_values.reshape(-1)
    gathered = jnp.zeros(atom_released_joules.shape, jnp.float32)
    for index in range(8):
        gathered = gathered + corners[index][3] * raveled_fresh[targets[index]]
    probe_warmth_readout = jnp.where(live, gathered, 0.0)
    return advanced_warmth_values, probe_warmth_readout
```

```python
import functools

import jax
import jax.numpy as jnp
from jax import lax
from jax.experimental import pallas as pl
from jax.experimental.pallas import tpu as pltpu
from jax.sharding import PartitionSpec as P

ITERS = 8
recombine_gain = 3.0
half_interval = 16.0
interval_length = 32.0
MESH_ID = pl.DeviceIdType.MESH
HIGHEST = lax.Precision.HIGHEST
ROUNDS = ITERS + 2


def step_kernel(
    ns,
    nb,
    layers,
    chunk,
    v_ref,
    k_ref,
    joules_ref,
    local_ref,
    anchor_ref,
    oxygen_ref,
    entries_ref,
    x_ref,
    probe_ref,
    coef,
    fields,
    vectors,
    halo_z,
    halo_x,
    face_x,
    sums,
    atoms_out,
    atoms_in,
    weight_zx,
    weight_y,
    read_out,
    read_in,
    halo_send,
    halo_recv,
    sum_send,
    sum_recv,
    atom_send,
    atom_recv,
    read_send,
    read_recv,
):
    s = lax.axis_index("slab")
    b = lax.axis_index("brick")
    rows, columns = v_ref.shape
    lines = rows // layers
    slots = joules_ref.shape[1]
    devices = ns * nb
    me = s * nb + b

    def wrapped(index, count):
        return jnp.where(index >= count, index - count, index)

    def for_peers(action):
        for shift in range(1, nb):
            action(s, wrapped(b + shift, nb))

        def outer(step, carry):
            for shift in range(nb):
                action(wrapped(s + step, ns), wrapped(b + shift, nb))
            return carry

        lax.fori_loop(1, ns, outer, 0)

    barrier = pltpu.get_barrier_semaphore()
    for_peers(
        lambda ps, pb: pl.semaphore_signal(
            barrier, inc=1, device_id=(ps, pb), device_id_type=MESH_ID
        )
    )

    low_slab, high_slab = s > 0, s < ns - 1
    low_brick, high_brick = b > 0, b < nb - 1

    @pl.when(s == 0)
    def _():
        halo_z[:, 0] = jnp.zeros_like(halo_z[:, 0])

    @pl.when(s == ns - 1)
    def _():
        halo_z[:, 1] = jnp.zeros_like(halo_z[:, 1])

    @pl.when(b == 0)
    def _():
        halo_x[:, 0] = jnp.zeros_like(halo_x[:, 0])

    @pl.when(b == nb - 1)
    def _():
        halo_x[:, 1] = jnp.zeros_like(halo_x[:, 1])

    def halo_parts(turn, block):
        top = pl.ds(rows - lines, lines)
        return (
            (high_slab, low_slab, block.at[top], halo_z.at[turn, 0], (s + 1, b)),
            (low_slab, high_slab, block.at[pl.ds(0, lines)], halo_z.at[turn, 1], (s - 1, b)),
            (high_brick, low_brick, face_x.at[turn, 0], halo_x.at[turn, 0], (s, b + 1)),
            (low_brick, high_brick, face_x.at[turn, 1], halo_x.at[turn, 1], (s, b - 1)),
        )

    def halo_copy(turn, way, source, target, device):
        return pltpu.make_async_remote_copy(
            src_ref=source,
            dst_ref=target,
            send_sem=halo_send.at[turn, way],
            recv_sem=halo_recv.at[turn, way],
            device_id=device,
            device_id_type=MESH_ID,
        )

    def stage_faces(turn, block):
        for z in range(layers):
            first, last = z * lines, z * lines + lines - 1
            face_x[turn, 0, pl.ds(z, 1), :] = block[pl.ds(last, 1), :]
            face_x[turn, 1, pl.ds(z, 1), :] = block[pl.ds(first, 1), :]

    def start_halo(turn, block):
        for way, (sends, _, source, target, device) in enumerate(halo_parts(turn, block)):

            @pl.when(sends)
            def _():
                halo_copy(turn, way, source, target, device).start()

    def wait_halo(turn, block):
        for way, (_, receives, source, target, device) in enumerate(halo_parts(turn, block)):

            @pl.when(receives)
            def _():
                halo_copy(turn, way, source, target, device).wait_recv()

    def end_halo(turn, block):
        for way, (sends, _, source, target, device) in enumerate(halo_parts(turn, block)):

            @pl.when(sends)
            def _():
                halo_copy(turn, way, source, target, device).wait_send()

    def atom_copy(peer, source, target, out_sem, in_sem):
        return pltpu.make_async_remote_copy(
            src_ref=source,
            dst_ref=target,
            send_sem=out_sem,
            recv_sem=in_sem,
            device_id=(peer, b),
            device_id_type=MESH_ID,
        )

    def for_slabs(action):
        def body(step, carry):
            action(wrapped(s + step, ns))
            return carry

        lax.fori_loop(1, ns, body, 0)

    row_of = lax.broadcasted_iota(jnp.int32, (ns, slots), 0)
    limit = jnp.zeros((ns, slots), jnp.int32)
    for owner in range(ns):
        limit = jnp.where(row_of == owner, entries_ref[owner], limit)
    live = lax.broadcasted_iota(jnp.int32, (ns, slots), 1) < limit
    heat = jnp.where(
        live,
        joules_ref[...] * (1.0 + recombine_gain * oxygen_ref[...].astype(jnp.float32)),
        0.0,
    )
    anchor = anchor_ref[...]
    line = anchor // columns
    column = (anchor - line * columns).astype(jnp.float32)
    line = line.astype(jnp.float32)
    for owner in range(ns):
        here = slice(owner, owner + 1)
        atoms_out[owner, 0:1, :] = heat[here]
        atoms_out[owner, 1:4, :] = local_ref[owner]
        atoms_out[owner, 4:5, :] = line[here]
        atoms_out[owner, 5:6, :] = column[here]
        atoms_out[owner, 6:8, :] = jnp.zeros((2, slots), jnp.float32)
    stage_faces(0, k_ref)
    stage_faces(1, v_ref)
    pl.semaphore_wait(barrier, devices - 1)

    for_slabs(
        lambda peer: atom_copy(
            peer, atoms_out.at[peer], atoms_in.at[s], atom_send, atom_recv
        ).start()
    )
    start_halo(0, k_ref)
    start_halo(1, v_ref)
    atoms_in[s] = atoms_out[s]
    others = pl.ds(0, ns - 1)
    atom_copy(
        wrapped(s + 1, ns), atoms_out.at[others], atoms_in.at[others], atom_send, atom_recv
    ).wait()

    line_at = lax.broadcasted_iota(jnp.int32, (rows, slots), 0).astype(jnp.float32)
    column_at = lax.broadcasted_iota(jnp.int32, (columns, slots), 0).astype(jnp.float32)

    def deposit(part, total):
        warmed = []
        for index in range(chunk):
            packed = atoms_in[part * chunk + index]
            fz, fx, fy = packed[1:2], packed[2:3], packed[3:4]
            off = line_at - packed[4:5]
            gz, gx = 1.0 - fz, 1.0 - fx
            plain = jnp.where(off == 0.0, gz * gx, 0.0)
            plain = jnp.where(off == 1.0, gz * fx, plain)
            plain = jnp.where(off == float(lines), fz * gx, plain)
            plain = jnp.where(off == float(lines + 1), fz * fx, plain)
            offy = column_at - packed[5:6]
            lane = pl.ds(index * slots, slots)
            weight_zx[part, :, lane] = plain
            weight_y[part, :, lane] = jnp.where(
                offy == 0.0, 1.0 - fy, jnp.where(offy == 1.0, fy, 0.0)
            )
            warmed.append(plain * packed[0:1])
        return total + lax.dot_general(
            jnp.concatenate(warmed, axis=1),
            weight_y[part],
            (((1,), (1,)), ((), ())),
            precision=HIGHEST,
            preferred_element_type=jnp.float32,
        )

    source = lax.fori_loop(
        0, ns // chunk, deposit, jnp.zeros((rows, columns), jnp.float32)
    )

    row = lax.broadcasted_iota(jnp.int32, (rows, columns), 0)
    col = lax.broadcasted_iota(jnp.int32, (rows, columns), 1)
    within = row % lines
    first_line, last_line = within == 0, within == lines - 1

    def neighbours(block, turn):
        low_z, high_z = halo_z[turn, 0], halo_z[turn, 1]
        below = jnp.concatenate([low_z, block[: rows - lines]], axis=0)
        above = jnp.concatenate([block[lines:], high_z], axis=0)
        low_x = jnp.concatenate(
            [
                jnp.broadcast_to(halo_x[turn, 0, pl.ds(z, 1), :], (lines, columns))
                for z in range(layers)
            ],
            axis=0,
        )
        high_x = jnp.concatenate(
            [
                jnp.broadcast_to(halo_x[turn, 1, pl.ds(z, 1), :], (lines, columns))
                for z in range(layers)
            ],
            axis=0,
        )
        left = jnp.where(first_line, low_x, pltpu.roll(block, 1, 0))
        right = jnp.where(last_line, high_x, pltpu.roll(block, rows - 1, 0))
        before = pltpu.roll(block, 1, 1)
        after = pltpu.roll(block, columns - 1, 1)
        return below, above, left, right, before, after

    def operator(block, turn):
        near = neighbours(block, turn)
        out = coef[6] * block
        for index in range(6):
            out = out - coef[index] * near[index]
        return out

    wait_halo(0, k_ref)
    k = k_ref[...]
    inside = (
        (row >= lines) | low_slab,
        (row < rows - lines) | high_slab,
        jnp.logical_not(first_line) | low_brick,
        jnp.logical_not(last_line) | high_brick,
        col > 0,
        col < columns - 1,
    )
    diagonal = jnp.zeros((rows, columns), jnp.float32)
    for index, other in enumerate(neighbours(k, 0)):
        face = (0.5 * half_interval) * (k + jnp.where(inside[index], other, 0.0))
        coef[index] = jnp.where(inside[index], face, 0.0)
        diagonal = diagonal + face
    coef[6] = 1.0 + diagonal

    wait_halo(1, v_ref)
    v = v_ref[...]
    near = neighbours(v, 1)
    spread = diagonal * v
    for index in range(6):
        spread = spread - coef[index] * near[index]
    residual = interval_length * source - 2.0 * spread
    fields[0] = residual
    stage_faces(2, fields.at[0])
    start_halo(2, fields.at[0])
    vectors[0] = residual
    x_ref[...] = v
    wait_halo(2, fields.at[0])
    fields[1] = operator(residual, 2)

    before_rr = None
    before_alpha = None
    for step in range(ITERS):
        last = step == ITERS - 1
        image = fields.at[step + 1]
        turn = step + 3
        if not last:
            stage_faces(turn, image)
            start_halo(turn, image)
        r = vectors[0]
        w = image[...]
        sums[step, me] = jnp.concatenate(
            [
                functools.reduce(
                    jnp.add,
                    [
                        jnp.sum(item, axis=0, keepdims=True)[:, at : at + 128]
                        for at in range(0, columns, 128)
                    ],
                )
                for item in (r * r, r * w)
            ],
            axis=0,
        )

        def sum_copy(part, ps, pb):
            return pltpu.make_async_remote_copy(
                src_ref=part,
                dst_ref=part,
                send_sem=sum_send.at[step],
                recv_sem=sum_recv.at[step],
                device_id=(ps, pb),
                device_id_type=MESH_ID,
            )

        for_peers(lambda ps, pb: sum_copy(sums.at[step, me], ps, pb).start())
        if not last:
            wait_halo(turn, image)
            q = operator(w, turn)
        sum_copy(
            sums.at[step, pl.ds(0, devices - 1)], wrapped(s + 1, ns), b
        ).wait()
        total = jnp.sum(
            jnp.sum(sums[step], axis=0), axis=1, keepdims=True
        )
        rr, rw = total[0:1], total[1:2]
        if step == 0:
            alpha = rr / rw
            p = r
            sp = w
            zp = q
        else:
            beta = rr / before_rr
            alpha = rr / (rw - beta * rr / before_alpha)
            p = r + beta * vectors[1]
            if not last:
                sp = w + beta * vectors[2]
                zp = q + beta * vectors[3]
        x_ref[...] = x_ref[...] + alpha * p
        if not last:
            vectors[0] = r - alpha * sp
            fields[step + 2] = w - alpha * zp
            vectors[1] = p
            vectors[2] = sp
            vectors[3] = zp
        before_rr, before_alpha = rr, alpha

    x = x_ref[...]

    def interpolate(part, carry):
        lifted = jnp.dot(
            x, weight_y[part], precision=HIGHEST, preferred_element_type=jnp.float32
        )
        read = jnp.sum(lifted * weight_zx[part], axis=0, keepdims=True)
        for index in range(chunk):
            read_out[part * chunk + index] = read[:, index * slots : (index + 1) * slots]
        return carry

    lax.fori_loop(0, ns // chunk, interpolate, 0)
    for_slabs(
        lambda peer: atom_copy(
            peer, read_out.at[peer], read_in.at[s], read_send, read_recv
        ).start()
    )
    read_in[s] = read_out[s]
    end_halo(0, k_ref)
    end_halo(1, v_ref)
    for turn in range(2, ROUNDS):
        end_halo(turn, fields.at[turn - 2])
    atom_copy(
        wrapped(s + 1, ns), read_out.at[others], read_in.at[others], read_send, read_recv
    ).wait()
    for owner in range(ns):
        probe_ref[owner : owner + 1, :] = jnp.where(
            live[owner : owner + 1], read_in[owner], 0.0
        )


def per_device(
    ns,
    nb,
    opening_warmth_values,
    thermal_diffusivity_field,
    atom_released_joules,
    atom_local_coordinates,
    atom_anchor_voxel,
    atom_oxygen_flag,
    live_entries_number,
):
    layers, lines, columns = opening_warmth_values.shape
    slots = atom_released_joules.shape[-1]
    rows = layers * lines
    chunk = 8 if ns % 8 == 0 else ns
    parts = ns // chunk
    f32 = jnp.float32
    vmem = pl.BlockSpec(memory_space=pltpu.VMEM)
    dma = pltpu.SemaphoreType.DMA
    x, probe = pl.pallas_call(
        functools.partial(step_kernel, ns, nb, layers, chunk),
        out_shape=(
            jax.ShapeDtypeStruct((rows, columns), f32),
            jax.ShapeDtypeStruct((ns, slots), f32),
        ),
        in_specs=[vmem] * 6 + [pl.BlockSpec(memory_space=pltpu.SMEM)],
        out_specs=(vmem, vmem),
        scratch_shapes=[
            pltpu.VMEM((7, rows, columns), f32),
            pltpu.VMEM((ITERS + 1, rows, columns), f32),
            pltpu.VMEM((4, rows, columns), f32),
            pltpu.VMEM((ROUNDS, 2, lines, columns), f32),
            pltpu.VMEM((ROUNDS, 2, layers, columns), f32),
            pltpu.VMEM((ROUNDS, 2, layers, columns), f32),
            pltpu.VMEM((ITERS, ns * nb, 2, 128), f32),
            pltpu.VMEM((ns, 8, slots), f32),
            pltpu.VMEM((ns, 8, slots), f32),
            pltpu.VMEM((parts, rows, chunk * slots), f32),
            pltpu.VMEM((parts, columns, chunk * slots), f32),
            pltpu.VMEM((ns, 1, slots), f32),
            pltpu.VMEM((ns, 1, slots), f32),
            dma((ROUNDS, 4)),
            dma((ROUNDS, 4)),
            dma((ITERS,)),
            dma((ITERS,)),
            dma,
            dma,
            dma,
            dma,
        ],
        compiler_params=pltpu.CompilerParams(
            collective_id=0, has_side_effects=True, vmem_limit_bytes=48 * 1024 * 1024
        ),
        name="heat_step",
    )(
        opening_warmth_values.reshape(rows, columns),
        thermal_diffusivity_field.reshape(rows, columns),
        atom_released_joules.reshape(ns, slots),
        atom_local_coordinates.reshape(ns, 3, slots),
        atom_anchor_voxel.reshape(ns, slots),
        atom_oxygen_flag.reshape(ns, slots),
        live_entries_number.reshape(ns),
    )
    return x.reshape(layers, lines, columns), probe.reshape(1, 1, ns, slots)


def solution(mesh):
    placed = (
        P("slab", "brick", None),
        P("slab", "brick", None),
        P("slab", "brick", None, None),
        P("slab", "brick", None, None, None),
        P("slab", "brick", None, None),
        P("slab", "brick", None, None),
        P("slab", "brick", None),
    )
    return jax.shard_map(
        functools.partial(per_device, mesh.shape["slab"], mesh.shape["brick"]),
        mesh=mesh,
        in_specs=placed,
        out_specs=(P("slab", "brick", None), P("slab", "brick", None, None)),
        check_vma=False,
    )
```

```python
import functools

import jax
import jax.numpy as jnp
from jax import lax
from jax.experimental import pallas as pl
from jax.experimental.pallas import tpu as pltpu
from jax.sharding import PartitionSpec as P

ITERS = 8
recombine_gain = 3.0
half_interval = 16.0
interval_length = 32.0
MESH_ID = pl.DeviceIdType.MESH
HIGHEST = lax.Precision.HIGHEST
ROUNDS = ITERS + 2


def step_kernel(
    ns,
    nb,
    layers,
    chunk,
    v_hbm,
    k_hbm,
    joules_ref,
    local_ref,
    anchor_ref,
    oxygen_ref,
    entries_ref,
    x_ref,
    probe_ref,
    coef,
    fields,
    vectors,
    halo_z,
    halo_x,
    face_x,
    sums,
    atoms_out,
    atoms_in,
    weight_zx,
    weight_y,
    read_out,
    read_in,
    v_ref,
    k_ref,
    halo_send,
    halo_recv,
    sum_send,
    sum_recv,
    atom_send,
    atom_recv,
    read_send,
    read_recv,
    load_sem,
):
    s = lax.axis_index("slab")
    b = lax.axis_index("brick")
    rows, columns = v_ref.shape
    lines = rows // layers
    slots = joules_ref.shape[1]
    devices = ns * nb
    me = s * nb + b

    load_k = pltpu.make_async_copy(k_hbm, k_ref, load_sem.at[0])
    load_v = pltpu.make_async_copy(v_hbm, v_ref, load_sem.at[1])
    load_k.start()
    load_v.start()

    def wrapped(index, count):
        return jnp.where(index >= count, index - count, index)

    def for_peers(action):
        for shift in range(1, nb):
            action(s, wrapped(b + shift, nb))

        def outer(step, carry):
            for shift in range(nb):
                action(wrapped(s + step, ns), wrapped(b + shift, nb))
            return carry

        lax.fori_loop(1, ns, outer, 0)

    barrier = pltpu.get_barrier_semaphore()
    for_peers(
        lambda ps, pb: pl.semaphore_signal(
            barrier, inc=1, device_id=(ps, pb), device_id_type=MESH_ID
        )
    )

    low_slab, high_slab = s > 0, s < ns - 1
    low_brick, high_brick = b > 0, b < nb - 1

    @pl.when(s == 0)
    def _():
        halo_z[:, 0] = jnp.zeros_like(halo_z[:, 0])

    @pl.when(s == ns - 1)
    def _():
        halo_z[:, 1] = jnp.zeros_like(halo_z[:, 1])

    @pl.when(b == 0)
    def _():
        halo_x[:, 0] = jnp.zeros_like(halo_x[:, 0])

    @pl.when(b == nb - 1)
    def _():
        halo_x[:, 1] = jnp.zeros_like(halo_x[:, 1])

    def halo_parts(turn, block):
        top = pl.ds(rows - lines, lines)
        return (
            (high_slab, low_slab, block.at[top], halo_z.at[turn, 0], (s + 1, b)),
            (low_slab, high_slab, block.at[pl.ds(0, lines)], halo_z.at[turn, 1], (s - 1, b)),
            (high_brick, low_brick, face_x.at[turn, 0], halo_x.at[turn, 0], (s, b + 1)),
            (low_brick, high_brick, face_x.at[turn, 1], halo_x.at[turn, 1], (s, b - 1)),
        )

    def halo_copy(turn, way, source, target, device):
        return pltpu.make_async_remote_copy(
            src_ref=source,
            dst_ref=target,
            send_sem=halo_send.at[turn, way],
            recv_sem=halo_recv.at[turn, way],
            device_id=device,
            device_id_type=MESH_ID,
        )

    def stage_faces(turn, block):
        for z in range(layers):
            first, last = z * lines, z * lines + lines - 1
            face_x[turn, 0, pl.ds(z, 1), :] = block[pl.ds(last, 1), :]
            face_x[turn, 1, pl.ds(z, 1), :] = block[pl.ds(first, 1), :]

    def start_halo(turn, block):
        for way, (sends, _, source, target, device) in enumerate(halo_parts(turn, block)):

            @pl.when(sends)
            def _():
                halo_copy(turn, way, source, target, device).start()

    def wait_halo(turn, block):
        for way, (_, receives, source, target, device) in enumerate(halo_parts(turn, block)):

            @pl.when(receives)
            def _():
                halo_copy(turn, way, source, target, device).wait_recv()

    def end_halo(turn, block):
        for way, (sends, _, source, target, device) in enumerate(halo_parts(turn, block)):

            @pl.when(sends)
            def _():
                halo_copy(turn, way, source, target, device).wait_send()

    def atom_copy(peer, source, target, out_sem, in_sem):
        return pltpu.make_async_remote_copy(
            src_ref=source,
            dst_ref=target,
            send_sem=out_sem,
            recv_sem=in_sem,
            device_id=(peer, b),
            device_id_type=MESH_ID,
        )

    def for_slabs(action):
        def body(step, carry):
            action(wrapped(s + step, ns))
            return carry

        lax.fori_loop(1, ns, body, 0)

    row_of = lax.broadcasted_iota(jnp.int32, (ns, slots), 0)
    limit = jnp.zeros((ns, slots), jnp.int32)
    for owner in range(ns):
        limit = jnp.where(row_of == owner, entries_ref[owner], limit)
    live = lax.broadcasted_iota(jnp.int32, (ns, slots), 1) < limit
    heat = jnp.where(
        live,
        joules_ref[...] * (1.0 + recombine_gain * oxygen_ref[...].astype(jnp.float32)),
        0.0,
    )
    anchor = anchor_ref[...]
    line = anchor // columns
    column = (anchor - line * columns).astype(jnp.float32)
    line = line.astype(jnp.float32)
    for owner in range(ns):
        here = slice(owner, owner + 1)
        atoms_out[owner, 0:1, :] = heat[here]
        for axis in range(3):
            atoms_out[owner, axis + 1 : axis + 2, :] = local_ref[axis, here]
        atoms_out[owner, 4:5, :] = line[here]
        atoms_out[owner, 5:6, :] = column[here]
        atoms_out[owner, 6:8, :] = jnp.zeros((2, slots), jnp.float32)
    load_k.wait()
    load_v.wait()
    stage_faces(0, k_ref)
    stage_faces(1, v_ref)
    pl.semaphore_wait(barrier, devices - 1)

    for_slabs(
        lambda peer: atom_copy(
            peer, atoms_out.at[peer], atoms_in.at[s], atom_send, atom_recv
        ).start()
    )
    start_halo(0, k_ref)
    start_halo(1, v_ref)
    atoms_in[s] = atoms_out[s]
    others = pl.ds(0, ns - 1)
    atom_copy(
        wrapped(s + 1, ns), atoms_out.at[others], atoms_in.at[others], atom_send, atom_recv
    ).wait()

    line_at = lax.broadcasted_iota(jnp.int32, (rows, slots), 0).astype(jnp.float32)
    column_at = lax.broadcasted_iota(jnp.int32, (columns, slots), 0).astype(jnp.float32)

    def deposit(part, total):
        warmed = []
        for index in range(chunk):
            packed = atoms_in[part * chunk + index]
            fz, fx, fy = packed[1:2], packed[2:3], packed[3:4]
            off = line_at - packed[4:5]
            gz, gx = 1.0 - fz, 1.0 - fx
            plain = jnp.where(off == 0.0, gz * gx, 0.0)
            plain = jnp.where(off == 1.0, gz * fx, plain)
            plain = jnp.where(off == float(lines), fz * gx, plain)
            plain = jnp.where(off == float(lines + 1), fz * fx, plain)
            offy = column_at - packed[5:6]
            lane = pl.ds(index * slots, slots)
            weight_zx[part, :, lane] = plain
            weight_y[part, :, lane] = jnp.where(
                offy == 0.0, 1.0 - fy, jnp.where(offy == 1.0, fy, 0.0)
            )
            warmed.append(plain * packed[0:1])
        return total + lax.dot_general(
            jnp.concatenate(warmed, axis=1),
            weight_y[part],
            (((1,), (1,)), ((), ())),
            precision=HIGHEST,
            preferred_element_type=jnp.float32,
        )

    source = lax.fori_loop(
        0, ns // chunk, deposit, jnp.zeros((rows, columns), jnp.float32)
    )

    row = lax.broadcasted_iota(jnp.int32, (rows, columns), 0)
    col = lax.broadcasted_iota(jnp.int32, (rows, columns), 1)
    within = row % lines
    first_line, last_line = within == 0, within == lines - 1

    def neighbours(block, turn):
        low_z, high_z = halo_z[turn, 0], halo_z[turn, 1]
        below = jnp.concatenate([low_z, block[: rows - lines]], axis=0)
        above = jnp.concatenate([block[lines:], high_z], axis=0)
        low_x = jnp.concatenate(
            [
                jnp.broadcast_to(halo_x[turn, 0, pl.ds(z, 1), :], (lines, columns))
                for z in range(layers)
            ],
            axis=0,
        )
        high_x = jnp.concatenate(
            [
                jnp.broadcast_to(halo_x[turn, 1, pl.ds(z, 1), :], (lines, columns))
                for z in range(layers)
            ],
            axis=0,
        )
        left = jnp.where(first_line, low_x, pltpu.roll(block, 1, 0))
        right = jnp.where(last_line, high_x, pltpu.roll(block, rows - 1, 0))
        before = pltpu.roll(block, 1, 1)
        after = pltpu.roll(block, columns - 1, 1)
        return below, above, left, right, before, after

    def operator(block, turn):
        near = neighbours(block, turn)
        out = coef[6] * block
        for index in range(6):
            out = out - coef[index] * near[index]
        return out

    wait_halo(0, k_ref)
    k = k_ref[...]
    inside = (
        (row >= lines) | low_slab,
        (row < rows - lines) | high_slab,
        jnp.logical_not(first_line) | low_brick,
        jnp.logical_not(last_line) | high_brick,
        col > 0,
        col < columns - 1,
    )
    diagonal = jnp.zeros((rows, columns), jnp.float32)
    for index, other in enumerate(neighbours(k, 0)):
        face = (0.5 * half_interval) * (k + jnp.where(inside[index], other, 0.0))
        coef[index] = jnp.where(inside[index], face, 0.0)
        diagonal = diagonal + face
    coef[6] = 1.0 + diagonal

    wait_halo(1, v_ref)
    v = v_ref[...]
    near = neighbours(v, 1)
    spread = diagonal * v
    for index in range(6):
        spread = spread - coef[index] * near[index]
    residual = interval_length * source - 2.0 * spread
    fields[0] = residual
    stage_faces(2, fields.at[0])
    start_halo(2, fields.at[0])
    vectors[0] = residual
    x_ref[...] = v
    wait_halo(2, fields.at[0])
    fields[1] = operator(residual, 2)

    def interpolate(part, carry):
        lifted = jnp.dot(
            jnp.concatenate([x_ref[...], vectors[0], vectors[1]], axis=0),
            weight_y[part],
            precision=HIGHEST,
            preferred_element_type=jnp.float32,
        )
        weights = weight_zx[part]
        for kind in range(3):
            read = jnp.sum(
                lifted[kind * rows : (kind + 1) * rows] * weights, axis=0, keepdims=True
            )
            for index in range(chunk):
                read_out[part * chunk + index, kind : kind + 1, :] = read[
                    :, index * slots : (index + 1) * slots
                ]
        return carry

    before_rr = None
    before_alpha = None
    for step in range(ITERS):
        last = step == ITERS - 1
        image = fields.at[step + 1]
        turn = step + 3
        r = vectors[0]
        w = image[...]
        sums[step, me] = jnp.concatenate(
            [
                functools.reduce(
                    jnp.add,
                    [
                        jnp.sum(item, axis=0, keepdims=True)[:, at : at + 128]
                        for at in range(0, columns, 128)
                    ],
                )
                for item in (r * r, r * w)
            ],
            axis=0,
        )

        def sum_copy(part, ps, pb):
            return pltpu.make_async_remote_copy(
                src_ref=part,
                dst_ref=part,
                send_sem=sum_send.at[step],
                recv_sem=sum_recv.at[step],
                device_id=(ps, pb),
                device_id_type=MESH_ID,
            )

        for_peers(lambda ps, pb: sum_copy(sums.at[step, me], ps, pb).start())
        if not last:
            stage_faces(turn, image)
            start_halo(turn, image)
            wait_halo(turn, image)
            q = operator(w, turn)
        else:
            lax.fori_loop(0, ns // chunk, interpolate, 0)
            for_slabs(
                lambda peer: atom_copy(
                    peer, read_out.at[peer], read_in.at[s], read_send, read_recv
                ).start()
            )
            read_in[s] = read_out[s]
        sum_copy(
            sums.at[step, pl.ds(0, devices - 1)], wrapped(s + 1, ns), b
        ).wait()
        total = jnp.sum(
            jnp.sum(sums[step], axis=0), axis=1, keepdims=True
        )
        rr, rw = total[0:1], total[1:2]
        if step == 0:
            alpha = rr / rw
            p = r
            sp = w
            zp = q
        else:
            beta = rr / before_rr
            alpha = rr / (rw - beta * rr / before_alpha)
            p = r + beta * vectors[1]
            if not last:
                sp = w + beta * vectors[2]
                zp = q + beta * vectors[3]
        x_ref[...] = x_ref[...] + alpha * p
        if not last:
            vectors[0] = r - alpha * sp
            fields[step + 2] = w - alpha * zp
            vectors[1] = p
            vectors[2] = sp
            vectors[3] = zp
        before_rr, before_alpha = rr, alpha

    end_halo(0, k_ref)
    end_halo(1, v_ref)
    for turn in range(2, ROUNDS):
        end_halo(turn, fields.at[turn - 2])
    atom_copy(
        wrapped(s + 1, ns), read_out.at[others], read_in.at[others], read_send, read_recv
    ).wait()
    for owner in range(ns):
        probe_ref[owner : owner + 1, :] = jnp.where(
            live[owner : owner + 1],
            read_in[owner, 0:1, :]
            + alpha * (read_in[owner, 1:2, :] + beta * read_in[owner, 2:3, :]),
            0.0,
        )


def per_device(
    ns,
    nb,
    opening_warmth_values,
    thermal_diffusivity_field,
    atom_released_joules,
    atom_local_coordinates,
    atom_anchor_voxel,
    atom_oxygen_flag,
    live_entries_number,
):
    layers, lines, columns = opening_warmth_values.shape
    slots = atom_released_joules.shape[-1]
    rows = layers * lines
    chunk = 8 if ns % 8 == 0 else ns
    parts = ns // chunk
    f32 = jnp.float32
    vmem = pl.BlockSpec(memory_space=pltpu.VMEM)
    dma = pltpu.SemaphoreType.DMA
    x, probe = pl.pallas_call(
        functools.partial(step_kernel, ns, nb, layers, chunk),
        out_shape=(
            jax.ShapeDtypeStruct((rows, columns), f32),
            jax.ShapeDtypeStruct((ns, slots), f32),
        ),
        in_specs=[pl.BlockSpec(memory_space=pl.ANY)] * 2
        + [vmem] * 4
        + [pl.BlockSpec(memory_space=pltpu.SMEM)],
        out_specs=(vmem, vmem),
        scratch_shapes=[
            pltpu.VMEM((7, rows, columns), f32),
            pltpu.VMEM((ITERS + 1, rows, columns), f32),
            pltpu.VMEM((4, rows, columns), f32),
            pltpu.VMEM((ROUNDS, 2, lines, columns), f32),
            pltpu.VMEM((ROUNDS, 2, layers, columns), f32),
            pltpu.VMEM((ROUNDS, 2, layers, columns), f32),
            pltpu.VMEM((ITERS, ns * nb, 2, 128), f32),
            pltpu.VMEM((ns, 8, slots), f32),
            pltpu.VMEM((ns, 8, slots), f32),
            pltpu.VMEM((parts, rows, chunk * slots), f32),
            pltpu.VMEM((parts, columns, chunk * slots), f32),
            pltpu.VMEM((ns, 3, slots), f32),
            pltpu.VMEM((ns, 3, slots), f32),
            pltpu.VMEM((rows, columns), f32),
            pltpu.VMEM((rows, columns), f32),
            dma((ROUNDS, 4)),
            dma((ROUNDS, 4)),
            dma((ITERS,)),
            dma((ITERS,)),
            dma,
            dma,
            dma,
            dma,
            dma((2,)),
        ],
        compiler_params=pltpu.CompilerParams(
            collective_id=0, has_side_effects=True, vmem_limit_bytes=48 * 1024 * 1024
        ),
        name="heat_step",
    )(
        opening_warmth_values.reshape(rows, columns),
        thermal_diffusivity_field.reshape(rows, columns),
        atom_released_joules.reshape(ns, slots),
        jnp.swapaxes(atom_local_coordinates.reshape(ns, 3, slots), 0, 1),
        atom_anchor_voxel.reshape(ns, slots),
        atom_oxygen_flag.reshape(ns, slots),
        live_entries_number.reshape(ns),
    )
    return x.reshape(layers, lines, columns), probe.reshape(1, 1, ns, slots)


def solution(mesh):
    placed = (
        P("slab", "brick", None),
        P("slab", "brick", None),
        P("slab", "brick", None, None),
        P("slab", "brick", None, None, None),
        P("slab", "brick", None, None),
        P("slab", "brick", None, None),
        P("slab", "brick", None),
    )
    return jax.shard_map(
        functools.partial(per_device, mesh.shape["slab"], mesh.shape["brick"]),
        mesh=mesh,
        in_specs=placed,
        out_specs=(P("slab", "brick", None), P("slab", "brick", None, None)),
        check_vma=False,
    )
```

```python
import functools

import jax
import jax.numpy as jnp
from jax import lax
from jax.experimental import pallas as pl
from jax.experimental.pallas import tpu as pltpu
from jax.sharding import PartitionSpec as P

ITERS = 8
recombine_gain = 3.0
half_interval = 16.0
interval_length = 32.0
MESH_ID = pl.DeviceIdType.MESH
HIGHEST = lax.Precision.HIGHEST
ROUNDS = ITERS + 2


def step_kernel(
    ns,
    nb,
    layers,
    chunk,
    v_hbm,
    k_hbm,
    joules_ref,
    local_ref,
    anchor_ref,
    oxygen_ref,
    entries_ref,
    x_ref,
    probe_ref,
    coef,
    fields,
    vectors,
    halo_z,
    halo_x,
    face_x,
    sums,
    atoms_out,
    atoms_in,
    weight_zx,
    weight_y,
    read_out,
    read_in,
    v_ref,
    k_ref,
    halo_send,
    halo_recv,
    sum_send,
    sum_recv,
    atom_send,
    atom_recv,
    read_send,
    read_recv,
    load_sem,
):
    s = lax.axis_index("slab")
    b = lax.axis_index("brick")
    rows, columns = v_ref.shape
    lines = rows // layers
    slots = joules_ref.shape[1]
    devices = ns * nb
    me = s * nb + b

    load_k = pltpu.make_async_copy(k_hbm, k_ref, load_sem.at[0])
    load_v = pltpu.make_async_copy(v_hbm, v_ref, load_sem.at[1])
    load_k.start()
    load_v.start()

    def wrapped(index, count):
        return jnp.where(index >= count, index - count, index)

    def for_peers(action):
        for shift in range(1, nb):
            action(s, wrapped(b + shift, nb))

        def outer(step, carry):
            for shift in range(nb):
                action(wrapped(s + step, ns), wrapped(b + shift, nb))
            return carry

        lax.fori_loop(1, ns, outer, 0)

    barrier = pltpu.get_barrier_semaphore()
    for_peers(
        lambda ps, pb: pl.semaphore_signal(
            barrier, inc=1, device_id=(ps, pb), device_id_type=MESH_ID
        )
    )

    low_slab, high_slab = s > 0, s < ns - 1
    low_brick, high_brick = b > 0, b < nb - 1

    @pl.when(s == 0)
    def _():
        halo_z[:, 0] = jnp.zeros_like(halo_z[:, 0])

    @pl.when(s == ns - 1)
    def _():
        halo_z[:, 1] = jnp.zeros_like(halo_z[:, 1])

    @pl.when(b == 0)
    def _():
        halo_x[:, 0] = jnp.zeros_like(halo_x[:, 0])

    @pl.when(b == nb - 1)
    def _():
        halo_x[:, 1] = jnp.zeros_like(halo_x[:, 1])

    def halo_parts(turn, block):
        top = pl.ds(rows - lines, lines)
        return (
            (high_slab, low_slab, block.at[top], halo_z.at[turn, 0], (s + 1, b)),
            (low_slab, high_slab, block.at[pl.ds(0, lines)], halo_z.at[turn, 1], (s - 1, b)),
            (high_brick, low_brick, face_x.at[turn, 0], halo_x.at[turn, 0], (s, b + 1)),
            (low_brick, high_brick, face_x.at[turn, 1], halo_x.at[turn, 1], (s, b - 1)),
        )

    def halo_copy(turn, way, source, target, device):
        return pltpu.make_async_remote_copy(
            src_ref=source,
            dst_ref=target,
            send_sem=halo_send.at[turn, way],
            recv_sem=halo_recv.at[turn, way],
            device_id=device,
            device_id_type=MESH_ID,
        )

    def stage_faces(turn, block):
        for z in range(layers):
            first, last = z * lines, z * lines + lines - 1
            face_x[turn, 0, pl.ds(z, 1), :] = block[pl.ds(last, 1), :]
            face_x[turn, 1, pl.ds(z, 1), :] = block[pl.ds(first, 1), :]

    def start_halo(turn, block):
        for way, (sends, _, source, target, device) in enumerate(halo_parts(turn, block)):

            @pl.when(sends)
            def _():
                halo_copy(turn, way, source, target, device).start()

    def wait_halo(turn, block):
        for way, (_, receives, source, target, device) in enumerate(halo_parts(turn, block)):

            @pl.when(receives)
            def _():
                halo_copy(turn, way, source, target, device).wait_recv()

    def end_halo(turn, block):
        for way, (sends, _, source, target, device) in enumerate(halo_parts(turn, block)):

            @pl.when(sends)
            def _():
                halo_copy(turn, way, source, target, device).wait_send()

    def atom_copy(peer, source, target, out_sem, in_sem):
        return pltpu.make_async_remote_copy(
            src_ref=source,
            dst_ref=target,
            send_sem=out_sem,
            recv_sem=in_sem,
            device_id=(peer, b),
            device_id_type=MESH_ID,
        )

    def for_slabs(action):
        def body(step, carry):
            action(wrapped(s + step, ns))
            return carry

        lax.fori_loop(1, ns, body, 0)

    row_of = lax.broadcasted_iota(jnp.int32, (ns, slots), 0)
    limit = jnp.zeros((ns, slots), jnp.int32)
    for owner in range(ns):
        limit = jnp.where(row_of == owner, entries_ref[owner], limit)
    live = lax.broadcasted_iota(jnp.int32, (ns, slots), 1) < limit
    heat = jnp.where(
        live,
        joules_ref[...] * (1.0 + recombine_gain * oxygen_ref[...].astype(jnp.float32)),
        0.0,
    )
    anchor = anchor_ref[...]
    line = anchor // columns
    column = (anchor - line * columns).astype(jnp.float32)
    line = line.astype(jnp.float32)
    for owner in range(ns):
        here = slice(owner, owner + 1)
        atoms_out[owner, 0:1, :] = heat[here]
        for axis in range(3):
            atoms_out[owner, axis + 1 : axis + 2, :] = local_ref[axis, here]
        atoms_out[owner, 4:5, :] = line[here]
        atoms_out[owner, 5:6, :] = column[here]
        atoms_out[owner, 6:8, :] = jnp.zeros((2, slots), jnp.float32)
    load_k.wait()
    load_v.wait()
    stage_faces(0, k_ref)
    stage_faces(1, v_ref)
    pl.semaphore_wait(barrier, devices - 1)

    for_slabs(
        lambda peer: atom_copy(
            peer, atoms_out.at[peer], atoms_in.at[s], atom_send, atom_recv
        ).start()
    )
    start_halo(0, k_ref)
    start_halo(1, v_ref)
    atoms_in[s] = atoms_out[s]
    others = pl.ds(0, ns - 1)
    atom_copy(
        wrapped(s + 1, ns), atoms_out.at[others], atoms_in.at[others], atom_send, atom_recv
    ).wait()

    line_at = lax.broadcasted_iota(jnp.int32, (rows, slots), 0).astype(jnp.float32)
    column_at = lax.broadcasted_iota(jnp.int32, (columns, slots), 0).astype(jnp.float32)

    def deposit(part, total):
        warmed = []
        for index in range(chunk):
            packed = atoms_in[part * chunk + index]
            fz, fx, fy = packed[1:2], packed[2:3], packed[3:4]
            off = line_at - packed[4:5]
            gz, gx = 1.0 - fz, 1.0 - fx
            plain = jnp.where(off == 0.0, gz * gx, 0.0)
            plain = jnp.where(off == 1.0, gz * fx, plain)
            plain = jnp.where(off == float(lines), fz * gx, plain)
            plain = jnp.where(off == float(lines + 1), fz * fx, plain)
            offy = column_at - packed[5:6]
            lane = pl.ds(index * slots, slots)
            weight_zx[part, :, lane] = plain
            weight_y[part, :, lane] = jnp.where(
                offy == 0.0, 1.0 - fy, jnp.where(offy == 1.0, fy, 0.0)
            )
            warmed.append(plain * packed[0:1])
        return total + lax.dot_general(
            jnp.concatenate(warmed, axis=1),
            weight_y[part],
            (((1,), (1,)), ((), ())),
            precision=HIGHEST,
            preferred_element_type=jnp.float32,
        )

    source = lax.fori_loop(
        0, ns // chunk, deposit, jnp.zeros((rows, columns), jnp.float32)
    )

    row = lax.broadcasted_iota(jnp.int32, (rows, columns), 0)
    col = lax.broadcasted_iota(jnp.int32, (rows, columns), 1)
    within = row % lines
    first_line, last_line = within == 0, within == lines - 1

    def neighbours(block, turn):
        low_z, high_z = halo_z[turn, 0], halo_z[turn, 1]
        below = jnp.concatenate([low_z, block[: rows - lines]], axis=0)
        above = jnp.concatenate([block[lines:], high_z], axis=0)
        low_x = jnp.concatenate(
            [
                jnp.broadcast_to(halo_x[turn, 0, pl.ds(z, 1), :], (lines, columns))
                for z in range(layers)
            ],
            axis=0,
        )
        high_x = jnp.concatenate(
            [
                jnp.broadcast_to(halo_x[turn, 1, pl.ds(z, 1), :], (lines, columns))
                for z in range(layers)
            ],
            axis=0,
        )
        left = jnp.where(first_line, low_x, pltpu.roll(block, 1, 0))
        right = jnp.where(last_line, high_x, pltpu.roll(block, rows - 1, 0))
        before = pltpu.roll(block, 1, 1)
        after = pltpu.roll(block, columns - 1, 1)
        return below, above, left, right, before, after

    def operator(block, turn):
        near = neighbours(block, turn)
        out = coef[6] * block
        for index in range(6):
            out = out - coef[index] * near[index]
        return out

    wait_halo(0, k_ref)
    k = k_ref[...]
    inside = (
        (row >= lines) | low_slab,
        (row < rows - lines) | high_slab,
        jnp.logical_not(first_line) | low_brick,
        jnp.logical_not(last_line) | high_brick,
        col > 0,
        col < columns - 1,
    )
    diagonal = jnp.zeros((rows, columns), jnp.float32)
    for index, other in enumerate(neighbours(k, 0)):
        face = (0.5 * half_interval) * (k + jnp.where(inside[index], other, 0.0))
        coef[index] = jnp.where(inside[index], face, 0.0)
        diagonal = diagonal + face
    coef[6] = 1.0 + diagonal

    wait_halo(1, v_ref)
    v = v_ref[...]
    near = neighbours(v, 1)
    spread = diagonal * v
    for index in range(6):
        spread = spread - coef[index] * near[index]
    residual = interval_length * source - 2.0 * spread
    fields[0] = residual
    stage_faces(2, fields.at[0])
    start_halo(2, fields.at[0])
    vectors[0] = residual
    x_ref[...] = v
    wait_halo(2, fields.at[0])
    fields[1] = operator(residual, 2)

    def interpolate(part, carry):
        lifted = jnp.dot(
            jnp.concatenate([x_ref[...], vectors[0], vectors[1]], axis=0),
            weight_y[part],
            precision=HIGHEST,
            preferred_element_type=jnp.float32,
        )
        weights = weight_zx[part]
        for kind in range(3):
            read = jnp.sum(
                lifted[kind * rows : (kind + 1) * rows] * weights, axis=0, keepdims=True
            )
            for index in range(chunk):
                read_out[part * chunk + index, kind : kind + 1, :] = read[
                    :, index * slots : (index + 1) * slots
                ]
        return carry

    left_half = lax.broadcasted_iota(jnp.int32, (1, 128), 1) < 64
    before_rr = None
    before_alpha = None
    for step in range(ITERS):
        last = step == ITERS - 1
        image = fields.at[step + 1]
        turn = step + 3
        r = vectors[0]
        w = image[...]
        narrow = [
            jnp.sum(
                functools.reduce(
                    jnp.add, [item[:, at : at + 128] for at in range(0, columns, 128)]
                ).reshape(rows // 8, 8, 128),
                axis=0,
            )
            for item in (r * r, r * w)
        ]
        sums[step, me] = jnp.sum(
            jnp.where(left_half, narrow[0], narrow[1])
            + pltpu.roll(jnp.where(left_half, narrow[1], narrow[0]), 64, 1),
            axis=0,
            keepdims=True,
        )

        def sum_copy(part, ps, pb):
            return pltpu.make_async_remote_copy(
                src_ref=part,
                dst_ref=part,
                send_sem=sum_send.at[step],
                recv_sem=sum_recv.at[step],
                device_id=(ps, pb),
                device_id_type=MESH_ID,
            )

        for_peers(lambda ps, pb: sum_copy(sums.at[step, me], ps, pb).start())
        if step > 0:
            x_ref[...] = x_ref[...] + before_alpha * vectors[1]
        if not last:
            stage_faces(turn, image)
            start_halo(turn, image)
            wait_halo(turn, image)
            q = operator(w, turn)
        else:
            lax.fori_loop(0, ns // chunk, interpolate, 0)
            for_slabs(
                lambda peer: atom_copy(
                    peer, read_out.at[peer], read_in.at[s], read_send, read_recv
                ).start()
            )
            read_in[s] = read_out[s]
        sum_copy(
            sums.at[step, pl.ds(0, devices - 1)], wrapped(s + 1, ns), b
        ).wait()
        total = jnp.sum(sums[step], axis=0)
        rr = jnp.sum(jnp.where(left_half, total, 0.0), axis=1, keepdims=True)
        rw = jnp.sum(jnp.where(left_half, 0.0, total), axis=1, keepdims=True)
        if step == 0:
            alpha = rr / rw
            p = r
            sp = w
            zp = q
        else:
            beta = rr / before_rr
            alpha = rr / (rw - beta * rr / before_alpha)
            p = r + beta * vectors[1]
            if not last:
                sp = w + beta * vectors[2]
                zp = q + beta * vectors[3]
        if last:
            x_ref[...] = x_ref[...] + alpha * p
        else:
            vectors[0] = r - alpha * sp
            fields[step + 2] = w - alpha * zp
            vectors[1] = p
            vectors[2] = sp
            vectors[3] = zp
        before_rr, before_alpha = rr, alpha

    end_halo(0, k_ref)
    end_halo(1, v_ref)
    for turn in range(2, ROUNDS):
        end_halo(turn, fields.at[turn - 2])
    atom_copy(
        wrapped(s + 1, ns), read_out.at[others], read_in.at[others], read_send, read_recv
    ).wait()
    for owner in range(ns):
        probe_ref[owner : owner + 1, :] = jnp.where(
            live[owner : owner + 1],
            read_in[owner, 0:1, :]
            + alpha * (read_in[owner, 1:2, :] + beta * read_in[owner, 2:3, :]),
            0.0,
        )


def per_device(
    ns,
    nb,
    opening_warmth_values,
    thermal_diffusivity_field,
    atom_released_joules,
    atom_local_coordinates,
    atom_anchor_voxel,
    atom_oxygen_flag,
    live_entries_number,
):
    layers, lines, columns = opening_warmth_values.shape
    slots = atom_released_joules.shape[-1]
    rows = layers * lines
    chunk = 8 if ns % 8 == 0 else ns
    parts = ns // chunk
    f32 = jnp.float32
    vmem = pl.BlockSpec(memory_space=pltpu.VMEM)
    dma = pltpu.SemaphoreType.DMA
    x, probe = pl.pallas_call(
        functools.partial(step_kernel, ns, nb, layers, chunk),
        out_shape=(
            jax.ShapeDtypeStruct((rows, columns), f32),
            jax.ShapeDtypeStruct((ns, slots), f32),
        ),
        in_specs=[pl.BlockSpec(memory_space=pl.ANY)] * 2
        + [vmem] * 4
        + [pl.BlockSpec(memory_space=pltpu.SMEM)],
        out_specs=(vmem, vmem),
        scratch_shapes=[
            pltpu.VMEM((7, rows, columns), f32),
            pltpu.VMEM((ITERS + 1, rows, columns), f32),
            pltpu.VMEM((4, rows, columns), f32),
            pltpu.VMEM((ROUNDS, 2, lines, columns), f32),
            pltpu.VMEM((ROUNDS, 2, layers, columns), f32),
            pltpu.VMEM((ROUNDS, 2, layers, columns), f32),
            pltpu.VMEM((ITERS, ns * nb, 1, 128), f32),
            pltpu.VMEM((ns, 8, slots), f32),
            pltpu.VMEM((ns, 8, slots), f32),
            pltpu.VMEM((parts, rows, chunk * slots), f32),
            pltpu.VMEM((parts, columns, chunk * slots), f32),
            pltpu.VMEM((ns, 3, slots), f32),
            pltpu.VMEM((ns, 3, slots), f32),
            pltpu.VMEM((rows, columns), f32),
            pltpu.VMEM((rows, columns), f32),
            dma((ROUNDS, 4)),
            dma((ROUNDS, 4)),
            dma((ITERS,)),
            dma((ITERS,)),
            dma,
            dma,
            dma,
            dma,
            dma((2,)),
        ],
        compiler_params=pltpu.CompilerParams(
            collective_id=0, has_side_effects=True, vmem_limit_bytes=48 * 1024 * 1024
        ),
        name="heat_step",
    )(
        opening_warmth_values.reshape(rows, columns),
        thermal_diffusivity_field.reshape(rows, columns),
        atom_released_joules.reshape(ns, slots),
        jnp.swapaxes(atom_local_coordinates.reshape(ns, 3, slots), 0, 1),
        atom_anchor_voxel.reshape(ns, slots),
        atom_oxygen_flag.reshape(ns, slots),
        live_entries_number.reshape(ns),
    )
    return x.reshape(layers, lines, columns), probe.reshape(1, 1, ns, slots)


def solution(mesh):
    placed = (
        P("slab", "brick", None),
        P("slab", "brick", None),
        P("slab", "brick", None, None),
        P("slab", "brick", None, None, None),
        P("slab", "brick", None, None),
        P("slab", "brick", None, None),
        P("slab", "brick", None),
    )
    return jax.shard_map(
        functools.partial(per_device, mesh.shape["slab"], mesh.shape["brick"]),
        mesh=mesh,
        in_specs=placed,
        out_specs=(P("slab", "brick", None), P("slab", "brick", None, None)),
        check_vma=False,
    )
```
